512 devices in a mesh: blk: 128 (over y_hi, z, x, core), grp: 4 (over y_lo).
Axes of the slice: x: 4, y: 8 (y_hi: 2, y_lo: 4; y = y_hi * 4 + y_lo), z: 8, core: 2. Of those that a mesh axis runs over, the one named last changes fastest.
Arguments:
- amplitudes: bfloat16 [1024, 4, 8192], P(None, 'grp', 'blk'), may hold values from -6 to 6
- ladder_ints: bfloat16 [32768, 32768], P('grp', 'blk'), may hold values from -0.09375 to 0.09375
- pair_irrep: int32 [32768], replicated, may hold values from 0 to 7, as said below
- occ_gap: float32 [1024], replicated, may hold values from 0.5 to 3
- vir_energy: float32 [32768], P('blk'), may hold values from 0.5 to 5
- pair_subset: int32 [512], replicated, may hold values from 0 to 1023, as said below
Outputs:
- update: bfloat16 [512, 32768], P('grp', 'blk')
The draws below stay inside these ranges and needn't reach their ends.
Inputs may be any that keep to these rules, and one draw needn't show every extreme that they name: `pair_subset`: the entries are distinct. `pair_irrep`: labels never fall along the pairs, so each irrep is one contiguous run of pairs, of uneven lengths; the first pair has label 0 and the last label 7.
All inputs are finite; a program needn't handle non-finite values.
Results may differ from the reference program's by a relative error of at most 0.001.
Values may be sent and summed in bfloat16 or wider, within the bound.
No kernel may reach another device: no remote copies, remote signals or barrier semaphores. Data moves between devices by JAX's collectives and lax.ppermute only.
A program may use at most 64 MiB of HBM per device.

```python
import math
import jax
import jax.numpy as jnp
from jax import lax

OCC = 512
OCC_ALL = 1024
IRREPS = 8
PAIR_COLS = 256
PAIRS = 32768
PAIR_ROWS = 8192
N_BLK = 128
N_GRP = 4


def draw_pair_subset(key, part):
    key = jax.random.fold_in(key, 1)
    return jax.random.permutation(key, OCC_ALL)[:OCC].astype(jnp.int32)


def draw_pair_irrep(key, part):
    key = jax.random.fold_in(key, 2)
    cuts = jnp.sort(jax.random.randint(key, (IRREPS - 1,), 1, PAIRS, dtype=jnp.int32))
    places = jnp.arange(PAIRS, dtype=jnp.int32)
    return jnp.sum((places[:, None] >= cuts[None, :]).astype(jnp.int32), axis=1).astype(jnp.int32)


def shard_levels(key, dims, shards, smallest, high):
    def one(dim, parts):
        draws = jax.random.uniform(jax.random.fold_in(jax.random.fold_in(key, 6), dim), (parts,), jnp.float32, smallest / len(shards), high / len(shards))
        return jnp.repeat(jnp.exp(draws), dims[dim] // parts).reshape((-1,) + (1,) * (len(dims) - dim - 1))

    loudness = one(*shards[0])
    for cut in shards[1:]:
        loudness = loudness * one(*cut)
    return loudness


def centred(stream_key, dims, spread, bound, cuts=(), kind=jnp.bfloat16):
    gain = shard_levels(stream_key, dims, cuts, -0.22, 0.18) if cuts else 1.0
    drawn = jax.random.normal(stream_key, dims, jnp.float32) * spread * gain
    return jnp.minimum(jnp.maximum(drawn, -bound), bound).astype(kind)


def setup_inputs(seed: int = 0) -> dict:
    splits = jax.random.split(jax.random.key(seed), 7)
    return {
        "amplitudes": centred(splits[0], (OCC_ALL, N_GRP, PAIR_ROWS), 1.0, 6.0, ((1, 4), (2, 128))),
        "ladder_ints": centred(splits[1], (PAIRS, PAIRS), (PAIRS // 8) ** -0.5, 0.09375, ((0, 4), (1, 128))),
        "pair_irrep": draw_pair_irrep(jax.random.fold_in(splits[6], 71), 0),
        "occ_gap": jnp.clip(jnp.exp(jax.random.uniform(splits[3], (OCC_ALL,), jnp.float32, math.log(0.5), math.log(3.0))), 0.5, 3.0),
        "vir_energy": jnp.clip(jnp.exp(math.log(5.0) - 2.3025851 * jax.random.uniform(splits[4], (PAIRS,), jnp.float32) ** shard_levels(splits[4], (PAIRS,), ((0, 128),), -0.2, 0.2)), 0.5, 5.0),
        "pair_subset": draw_pair_subset(jax.random.fold_in(splits[6], 71), 0),
    }


def reference(amplitudes, ladder_ints, pair_irrep, occ_gap, vir_energy, pair_subset):
    chosen = jnp.take(amplitudes, pair_subset, axis=0).reshape(OCC, PAIRS)
    gaps = jnp.take(occ_gap, pair_subset)

    def column_block(position):
        begin = (position * PAIR_COLS).astype(jnp.int32)
        columns = lax.dynamic_slice_in_dim(ladder_ints, begin, PAIR_COLS, 1)
        col_irrep = lax.dynamic_slice_in_dim(pair_irrep, begin, PAIR_COLS, 0)
        masked = jnp.where(pair_irrep[:, None] == col_irrep[None, :], columns, jnp.zeros_like(columns))
        return jnp.dot(chosen, masked, preferred_element_type=jnp.float32)

    blocks = lax.map(column_block, jnp.arange(N_BLK, dtype=jnp.int32))
    ladder = jnp.transpose(blocks, (1, 0, 2)).reshape(OCC, PAIRS)
    denom = gaps[:, None] + vir_energy[None, :]
    return (ladder / denom).astype(jnp.bfloat16)
```

```python
import functools

import jax
import jax.numpy as jnp
from jax import lax
from jax.experimental import pallas as pl
from jax.experimental.pallas import tpu as pltpu
from jax.sharding import PartitionSpec as P

H, Z, X, C = 2, 8, 4, 2
SHARD = 64
OCC = 512
QUARTER = 8192
COLS = 256
GRP = 4
OWN = OCC // GRP
VMEM_LIMIT = 50 * 1024 * 1024


def index(h, z, x, c):
    return ((h % H * Z + z % Z) * X + x % X) * C + c


def devices():
    return [(h, z, x, c) for h in range(H) for z in range(Z) for x in range(X) for c in range(C)]


def groups():
    first = [[index(h, z, x, 0) for h in range(H) for x in range(X)] for z in range(Z)]
    second = [[index(h, z, x, 1) for z in range(Z)] for h in range(H) for x in range(X)]
    return first + second


def ring(step, cores=(0, 1)):
    pairs = []
    for h, z, x, c in devices():
        if c in cores:
            target = index(h, z + step, x, 0) if c == 0 else index(h, z, x + step, 1)
            pairs.append((index(h, z, x, c), target))
    return pairs


def across_h():
    return [(index(h, z, x, 1), index(h + 1, z, x, 1)) for h, z, x, c in devices() if c == 1]


def across_core():
    return [(index(h, z, x, c), index(h, z, x, 1 - c)) for h, z, x, c in devices()]


def select_kernel(amp_ref, subset_ref, out_ref):
    rows = amp_ref.shape[1]
    hot = (lax.broadcasted_iota(jnp.int32, (rows, OCC), 0) == subset_ref[...]).astype(jnp.bfloat16)
    chosen = jnp.dot(amp_ref[...], hot, preferred_element_type=jnp.float32).astype(jnp.bfloat16)
    for copy in range(8):
        out_ref[pl.ds(copy * SHARD, SHARD), :] = chosen


def select(amplitudes, subset):
    return pl.pallas_call(
        select_kernel,
        out_shape=jax.ShapeDtypeStruct((8 * SHARD, OCC), jnp.bfloat16),
        in_specs=[pl.BlockSpec(memory_space=pltpu.VMEM)] * 2,
        out_specs=pl.BlockSpec(memory_space=pltpu.VMEM),
        compiler_params=pltpu.CompilerParams(vmem_limit_bytes=VMEM_LIMIT),
        name="select",
    )(amplitudes, subset)


def ladder_kernel(place_ref, *refs):
    pieces, (plus4_ref, minus4_ref, across_ref, ints_ref, got_ref, low_ref, high_ref, out_ref, last_ref, acc_ref) = refs[:7], refs[7:]
    core = place_ref[64]
    start = place_ref[65]

    @pl.when(core == 0)
    def _():
        last_ref[pl.ds(0, 256), :] = plus4_ref[...]
        last_ref[pl.ds(256, 256), :] = minus4_ref[...]

    @pl.when(core == 1)
    def _():
        last_ref[...] = across_ref[...]

    low, high = low_ref[...], high_ref[...]
    for number, piece_ref in enumerate(pieces + (last_ref,)):
        parts = []
        for chunk in range(8):
            shard = place_ref[number * 8 + chunk]
            here = pl.multiple_of((2 * shard + core) * SHARD, SHARD)
            there = pl.multiple_of(shard * SHARD, SHARD)
            values = jnp.concatenate([ints_ref[pl.ds(here, SHARD), :], got_ref[pl.ds(there, SHARD), :]], axis=1)
            row = start + here + lax.broadcasted_iota(jnp.int32, values.shape, 0)
            keep = (row >= low) & (row < high)
            parts.append(jnp.where(keep, values, jnp.zeros_like(values)))
        masked = jnp.concatenate(parts, axis=0)
        term = lax.dot_general(masked, piece_ref[...], (((0,), (0,)), ((), ())), preferred_element_type=jnp.float32)
        if number == 0:
            acc_ref[...] = term
        else:
            acc_ref[...] += term
    for half in range(2):
        for owner in range(GRP):
            out_ref[half, owner] = acc_ref[pl.ds(half * COLS, COLS), pl.ds(owner * OWN, OWN)]


def ladder(place, pieces, plus4, minus4, across, ints, got, low, high):
    vmem = pl.BlockSpec(memory_space=pltpu.VMEM)
    return pl.pallas_call(
        ladder_kernel,
        out_shape=jax.ShapeDtypeStruct((2, GRP, COLS, OWN), jnp.float32),
        in_specs=[pl.BlockSpec(memory_space=pltpu.SMEM)] + [vmem] * 14,
        out_specs=vmem,
        scratch_shapes=[pltpu.VMEM((512, OCC), jnp.bfloat16), pltpu.VMEM((2 * COLS, OCC), jnp.float32)],
        compiler_params=pltpu.CompilerParams(vmem_limit_bytes=VMEM_LIMIT),
        cost_estimate=pl.CostEstimate(flops=2 * 512 * 512 * 4096, bytes_accessed=11 << 20, transcendentals=0),
        name="ladder",
    )(place, *pieces, plus4, minus4, across, ints, got, low, high)


def deal_kernel(me_ref, mine_ref, other_ref, *out_refs):
    me = me_ref[0]
    for step, out_ref in enumerate(out_refs):
        owner = lax.rem(me + step, GRP)
        out_ref[...] = mine_ref[0, owner] + other_ref[owner]


def deal(me, mine, other):
    vmem = pl.BlockSpec(memory_space=pltpu.VMEM)
    return pl.pallas_call(
        deal_kernel,
        out_shape=[jax.ShapeDtypeStruct((COLS, OWN), jnp.float32)] * GRP,
        in_specs=[pl.BlockSpec(memory_space=pltpu.SMEM), vmem, vmem],
        out_specs=[vmem] * GRP,
        compiler_params=pltpu.CompilerParams(vmem_limit_bytes=VMEM_LIMIT),
        name="deal",
    )(me, mine, other)


def close_kernel(a_ref, b_ref, c_ref, d_ref, gap_ref, vir_ref, out_ref):
    total = a_ref[...] + b_ref[...] + c_ref[...] + d_ref[...]
    out_ref[...] = (total.T / (gap_ref[...] + vir_ref[...])).astype(jnp.bfloat16)


def close(terms, gaps, vir):
    vmem = pl.BlockSpec(memory_space=pltpu.VMEM)
    return pl.pallas_call(
        close_kernel,
        out_shape=jax.ShapeDtypeStruct((OWN, COLS), jnp.bfloat16),
        in_specs=[vmem] * 6,
        out_specs=vmem,
        compiler_params=pltpu.CompilerParams(vmem_limit_bytes=VMEM_LIMIT),
        name="close",
    )(*terms, gaps, vir)


def body(amplitudes, ladder_ints, pair_irrep, occ_gap, vir_energy, pair_subset):
    me = lax.axis_index("grp").astype(jnp.int32)
    blk = lax.axis_index("blk").astype(jnp.int32)
    c = blk % 2
    x = blk // 2 % X
    z = blk // 8 % Z
    h = blk // 64
    permute = functools.partial(lax.ppermute, axis_name="blk")

    amp = jnp.transpose(amplitudes[:, 0, :])
    copies = select(amp, pair_subset[None, :])
    own = lax.all_to_all(copies, "blk", 0, 0, axis_index_groups=groups(), tiled=True)

    pairs = ladder_ints.reshape(64, 2, SHARD, COLS)
    away = lax.dynamic_index_in_dim(pairs, 1 - c, axis=1, keepdims=False).reshape(64 * SHARD, COLS)
    got = permute(away, perm=across_core())

    plus, minus = ring(1), ring(-1)
    across = permute(own, perm=across_h())
    p1 = permute(own, perm=plus)
    m1 = permute(own, perm=minus)
    p2 = permute(p1, perm=plus)
    m2 = permute(jnp.where(c == 0, m1, across), perm=minus)
    p3 = permute(jnp.where(c == 0, p2, across), perm=plus)
    m3 = permute(m2, perm=minus)
    p4 = permute(p3[:256], perm=ring(1, (0,)))
    m4 = permute(m3[256:], perm=ring(-1, (0,)))

    t = jnp.arange(8, dtype=jnp.int32)
    z_from = [z, z - 1, z + 1, z - 2, z + 2, z - 3, z + 3, z + 4]
    zeros = [(t // 4 * Z + zz % Z) * X + t % 4 for zz in z_from]
    hx_from = [(h, x), (h, x - 1), (h, x + 1), (h, x - 2), (h + 1, x + 1), (h + 1, x - 1), (h + 1, x + 2), (h + 1, x)]
    ones = [(hh % H * Z + t) * X + xx % X for hh, xx in hx_from]
    shards = jnp.where(c == 0, jnp.concatenate(zeros), jnp.concatenate(ones))
    place = jnp.concatenate([shards, c[None], (me * QUARTER)[None]]).astype(jnp.int32)

    counts = jnp.sum((pair_irrep[None, :] < jnp.arange(9, dtype=jnp.int32)[:, None]).astype(jnp.int32), axis=1)
    labels = jnp.concatenate([
        lax.dynamic_slice_in_dim(pair_irrep, blk * COLS, COLS, 0),
        lax.dynamic_slice_in_dim(pair_irrep, (blk + 1 - 2 * c) * COLS, COLS, 0),
    ])
    is_label = labels[None, :] == jnp.arange(8, dtype=jnp.int32)[:, None]
    low = jnp.sum(jnp.where(is_label, counts[:8, None], 0), axis=0)[None, :]
    high = jnp.sum(jnp.where(is_label, counts[1:, None], 0), axis=0)[None, :]

    parts = ladder(place, (own, p1, m1, p2, m2, p3, m3), p4, m4, across, ladder_ints, got, low, high)
    other = permute(parts[1], perm=across_core())
    dealt = deal(me[None], parts, other)
    terms = [dealt[0]] + [
        lax.ppermute(dealt[step], "grp", [(i, (i + step) % GRP) for i in range(GRP)]) for step in range(1, GRP)
    ]
    own_subset = lax.dynamic_slice_in_dim(pair_subset, me * OWN, OWN, 0)
    gaps = jnp.take(occ_gap, own_subset)
    return close(terms, gaps[:, None], vir_energy[None, :])


def solution(mesh):
    return jax.shard_map(
        body,
        mesh=mesh,
        in_specs=(P(None, "grp", "blk"), P("grp", "blk"), P(), P(), P("blk"), P()),
        out_specs=P("grp", "blk"),
        check_vma=False,
    )
```

```python
import functools

import jax
import jax.numpy as jnp
from jax import lax
from jax.experimental import pallas as pl
from jax.experimental.pallas import tpu as pltpu
from jax.sharding import PartitionSpec as P

H, Z, X, C = 2, 8, 4, 2
SHARD = 64
OCC = 512
QUARTER = 8192
COLS = 256
GRP = 4
OWN = OCC // GRP
VMEM_LIMIT = 16 * 1024 * 1024
STAGES = ((0, 1, 2), (3, 4), (5, 6), (7,))


def index(h, z, x, c):
    return ((h % H * Z + z % Z) * X + x % X) * C + c


def devices():
    return [(h, z, x, c) for h in range(H) for z in range(Z) for x in range(X) for c in range(C)]


def groups():
    first = [[index(h, z, x, 0) for h in range(H) for x in range(X)] for z in range(Z)]
    second = [[index(h, z, x, 1) for z in range(Z)] for h in range(H) for x in range(X)]
    return first + second


def ring(step, cores=(0, 1)):
    pairs = []
    for h, z, x, c in devices():
        if c in cores:
            target = index(h, z + step, x, 0) if c == 0 else index(h, z, x + step, 1)
            pairs.append((index(h, z, x, c), target))
    return pairs


def across_h():
    return [(index(h, z, x, 1), index(h + 1, z, x, 1)) for h, z, x, c in devices() if c == 1]


def across_core():
    return [(index(h, z, x, c), index(h, z, x, 1 - c)) for h, z, x, c in devices()]


def select_kernel(amp_ref, subset_ref, out_ref, held_ref, amp_here, subset_here, sems):
    fetch = [
        pltpu.make_async_copy(amp_ref, amp_here, sems.at[8]),
        pltpu.make_async_copy(subset_ref, subset_here, sems.at[9]),
    ]
    for copy in fetch:
        copy.start()
    for copy in fetch:
        copy.wait()
    rows = amp_here.shape[1]
    hot = (lax.broadcasted_iota(jnp.int32, (rows, OCC), 0) == subset_here[...]).astype(jnp.bfloat16)
    held_ref[...] = jnp.dot(amp_here[...], hot, preferred_element_type=jnp.float32).astype(jnp.bfloat16)
    copies = [
        pltpu.make_async_copy(held_ref, out_ref.at[pl.ds(copy * SHARD, SHARD), :], sems.at[copy]) for copy in range(8)
    ]
    for copy in copies:
        copy.start()
    for copy in copies:
        copy.wait()


def select(amplitudes, subset):
    return pl.pallas_call(
        select_kernel,
        out_shape=jax.ShapeDtypeStruct((8 * SHARD, OCC), jnp.bfloat16),
        in_specs=[pl.BlockSpec(memory_space=pltpu.HBM)] * 2,
        out_specs=pl.BlockSpec(memory_space=pltpu.HBM),
        scratch_shapes=[
            pltpu.VMEM((SHARD, OCC), jnp.bfloat16),
            pltpu.VMEM(amplitudes.shape, amplitudes.dtype),
            pltpu.VMEM(subset.shape, subset.dtype),
            pltpu.SemaphoreType.DMA((10,)),
        ],
        compiler_params=pltpu.CompilerParams(vmem_limit_bytes=VMEM_LIMIT),
        name="select",
    )(amplitudes, subset)


def pick_kernel(core_ref, first_ref, second_ref, out_ref):
    @pl.when(core_ref[0] == 0)
    def _():
        out_ref[...] = first_ref[...]

    @pl.when(core_ref[0] == 1)
    def _():
        out_ref[...] = second_ref[...]


def pick(core, first, second):
    vmem = pl.BlockSpec(memory_space=pltpu.VMEM)
    return pl.pallas_call(
        pick_kernel,
        out_shape=jax.ShapeDtypeStruct(first.shape, first.dtype),
        in_specs=[pl.BlockSpec(memory_space=pltpu.SMEM), vmem, vmem],
        out_specs=vmem,
        compiler_params=pltpu.CompilerParams(vmem_limit_bytes=VMEM_LIMIT),
        name="pick",
    )(core, first, second)


def prepare_kernel(place_ref, ints_ref, low_ref, high_ref, *out_refs):
    core = place_ref[64]
    start = place_ref[65]
    low, high = low_ref[...], high_ref[...]
    for number in range(8):
        parts = []
        for chunk in range(8):
            shard = place_ref[number * 8 + chunk]
            here = pl.multiple_of((2 * shard + core) * SHARD, SHARD)
            values = ints_ref[pl.ds(here, SHARD), :]
            row = start + here + lax.broadcasted_iota(jnp.int32, values.shape, 0)
            keep = (row >= low) & (row < high)
            parts.append(jnp.where(keep, values, jnp.zeros_like(values)))
        for stage, numbers in enumerate(STAGES):
            if number in numbers:
                out_refs[stage][number - numbers[0]] = jnp.concatenate(parts, axis=0).T


def prepare(place, ints, low, high):
    vmem = pl.BlockSpec(memory_space=pltpu.VMEM)
    return pl.pallas_call(
        prepare_kernel,
        out_shape=[jax.ShapeDtypeStruct((len(numbers), COLS, 512), jnp.bfloat16) for numbers in STAGES],
        in_specs=[pl.BlockSpec(memory_space=pltpu.SMEM)] + [vmem] * 3,
        out_specs=[vmem] * len(STAGES),
        compiler_params=pltpu.CompilerParams(vmem_limit_bytes=VMEM_LIMIT),
        cost_estimate=pl.CostEstimate(flops=0, bytes_accessed=12 << 20, transcendentals=0),
        name="prepare",
    )(place, ints, low, high)


def early_kernel(count, fresh, near_ref, far_ref, *refs):
    pieces, out_ref = refs[:count], refs[-1]
    for half, masked_ref in enumerate((near_ref, far_ref)):
        rows = pl.ds(half * COLS, COLS)
        total = None if fresh else refs[-2][rows, :]
        for at in range(count):
            term = jnp.dot(masked_ref[at], pieces[at][...], preferred_element_type=jnp.float32)
            total = term if total is None else total + term
        out_ref[rows, :] = total


def early(near, far, pieces, before=None):
    vmem = pl.BlockSpec(memory_space=pltpu.VMEM)
    inputs = (near, far, *pieces) + (() if before is None else (before,))
    return pl.pallas_call(
        functools.partial(early_kernel, len(pieces), before is None),
        out_shape=jax.ShapeDtypeStruct((2 * COLS, OCC), jnp.float32),
        in_specs=[vmem] * len(inputs),
        out_specs=vmem,
        compiler_params=pltpu.CompilerParams(vmem_limit_bytes=VMEM_LIMIT),
        cost_estimate=pl.CostEstimate(
            flops=len(pieces) * 2 * 512**3, bytes_accessed=len(pieces) << 20, transcendentals=0
        ),
        name="early",
    )(*inputs)


def tail_kernel(near_ref, far_ref, piece_ref, before_ref, mine_ref, away_ref):
    for half, (masked_ref, out_ref) in enumerate(((near_ref, mine_ref), (far_ref, away_ref))):
        total = before_ref[pl.ds(half * COLS, COLS), :]
        total += jnp.dot(masked_ref[0], piece_ref[...], preferred_element_type=jnp.float32)
        for owner in range(GRP):
            out_ref[owner] = total[:, owner * OWN : (owner + 1) * OWN]


def tail(near, far, piece, before):
    vmem = pl.BlockSpec(memory_space=pltpu.VMEM)
    return pl.pallas_call(
        tail_kernel,
        out_shape=[jax.ShapeDtypeStruct((GRP, COLS, OWN), jnp.float32)] * 2,
        in_specs=[vmem] * 4,
        out_specs=[vmem] * 2,
        compiler_params=pltpu.CompilerParams(vmem_limit_bytes=VMEM_LIMIT),
        cost_estimate=pl.CostEstimate(flops=2 * 512**3, bytes_accessed=4 << 20, transcendentals=0),
        name="tail",
    )(near, far, piece, before)


def deal_kernel(me_ref, mine_ref, other_ref, *out_refs):
    me = me_ref[0]
    for step, out_ref in enumerate(out_refs):
        owner = me ^ step
        out_ref[...] = mine_ref[owner] + other_ref[owner]


def deal(me, mine, other):
    vmem = pl.BlockSpec(memory_space=pltpu.VMEM)
    return pl.pallas_call(
        deal_kernel,
        out_shape=[jax.ShapeDtypeStruct((COLS, OWN), jnp.float32)] * GRP,
        in_specs=[pl.BlockSpec(memory_space=pltpu.SMEM), vmem, vmem],
        out_specs=[vmem] * GRP,
        compiler_params=pltpu.CompilerParams(vmem_limit_bytes=VMEM_LIMIT),
        name="deal",
    )(me, mine, other)


def close_kernel(a_ref, b_ref, c_ref, d_ref, gap_ref, vir_ref, out_ref):
    total = a_ref[...] + b_ref[...] + c_ref[...] + d_ref[...]
    out_ref[...] = (total.T / (gap_ref[...] + vir_ref[...])).astype(jnp.bfloat16)


def close(terms, gaps, vir):
    vmem = pl.BlockSpec(memory_space=pltpu.VMEM)
    return pl.pallas_call(
        close_kernel,
        out_shape=jax.ShapeDtypeStruct((OWN, COLS), jnp.bfloat16),
        in_specs=[vmem] * 6,
        out_specs=vmem,
        compiler_params=pltpu.CompilerParams(vmem_limit_bytes=VMEM_LIMIT),
        name="close",
    )(*terms, gaps, vir)


def body(amplitudes, ladder_ints, pair_irrep, occ_gap, vir_energy, pair_subset):
    me = lax.axis_index("grp").astype(jnp.int32)
    blk = lax.axis_index("blk").astype(jnp.int32)
    c = blk % 2
    x = blk // 2 % X
    z = blk // 8 % Z
    h = blk // 64
    permute = functools.partial(lax.ppermute, axis_name="blk")

    amp = jnp.transpose(amplitudes[:, 0, :])
    copies = select(amp, pair_subset[None, :])
    pair_irrep, ints, copies = lax.optimization_barrier((pair_irrep, ladder_ints, copies))
    got = permute(ints, perm=across_core())
    t = jnp.arange(8, dtype=jnp.int32)
    z_from = [z, z - 1, z + 1, z - 2, z + 2, z - 3, z + 3, z + 4]
    zeros = [(t // 4 * Z + zz % Z) * X + t % 4 for zz in z_from]
    hx_from = [(h, x), (h, x - 1), (h, x + 1), (h, x - 2), (h + 1, x), (h + 1, x - 1), (h + 1, x + 1), (h + 1, x + 2)]
    ones = [(hh % H * Z + t) * X + xx % X for hh, xx in hx_from]
    shards = jnp.where(c == 0, jnp.concatenate(zeros), jnp.concatenate(ones))
    place = jnp.concatenate([shards, c[None], (me * QUARTER)[None]]).astype(jnp.int32)

    counts = jnp.sum((pair_irrep[None, :] < jnp.arange(9, dtype=jnp.int32)[:, None]).astype(jnp.int32), axis=1)
    labels = jnp.concatenate([
        lax.dynamic_slice_in_dim(pair_irrep, blk * COLS, COLS, 0),
        lax.dynamic_slice_in_dim(pair_irrep, (blk + 1 - 2 * c) * COLS, COLS, 0),
    ])
    is_label = labels[None, :] == jnp.arange(8, dtype=jnp.int32)[:, None]
    low = jnp.sum(jnp.where(is_label, counts[:8, None], 0), axis=0)[None, :]
    high = jnp.sum(jnp.where(is_label, counts[1:, None], 0), axis=0)[None, :]

    own = lax.all_to_all(copies, "blk", 0, 0, axis_index_groups=groups(), tiled=True)
    near = prepare(place, ladder_ints, low[:, :COLS], high[:, :COLS])
    own, near = lax.optimization_barrier((own, near))
    plus, minus = ring(1), ring(-1)
    p1 = permute(own, perm=plus)
    m1 = permute(own, perm=minus)
    across = permute(own, perm=across_h())
    far = prepare(place, got, low[:, COLS:], high[:, COLS:])
    p2 = permute(p1, perm=plus)
    m2 = permute(m1, perm=ring(-1, (0,)))
    so_far = early(near[0], far[0], (own, p1, m1))
    p3_from = pick(c[None], p2, across)
    m3_from = pick(c[None], m2, across)
    p3 = permute(p3_from, perm=plus)
    p3, so_far = lax.optimization_barrier((p3, so_far))
    m3 = permute(m3_from, perm=minus)
    so_far = early(near[1], far[1], (p2, m3_from), so_far)
    p4 = permute(p3, perm=plus)
    so_far = early(near[2], far[2], (p3, m3), so_far)
    own_subset = lax.dynamic_slice_in_dim(pair_subset, me * OWN, OWN, 0)
    gaps = jnp.take(occ_gap, own_subset)
    so_far, gaps = lax.optimization_barrier((so_far, gaps))
    mine, away = tail(near[3], far[3], p4, so_far)
    other = permute(away, perm=across_core())
    dealt = deal(me[None], mine, other)
    terms = [dealt[0]]
    for step in (3, 2, 1):
        terms.append(lax.ppermute(dealt[step], "grp", [(i, i ^ step) for i in range(GRP)]))
    return close(terms, gaps[:, None], vir_energy[None, :])


def solution(mesh):
    return jax.shard_map(
        body,
        mesh=mesh,
        in_specs=(P(None, "grp", "blk"), P("grp", "blk"), P(), P(), P("blk"), P()),
        out_specs=P("grp", "blk"),
        check_vma=False,
    )
```

```python
import functools

import jax
import jax.numpy as jnp
from jax import lax
from jax.experimental import pallas as pl
from jax.experimental.pallas import tpu as pltpu
from jax.sharding import PartitionSpec as P

H, Z, X, C = 2, 8, 4, 2
SHARD = 64
OCC = 512
QUARTER = 8192
COLS = 256
GRP = 4
OWN = OCC // GRP
VMEM_LIMIT = 12 * 1024 * 1024
STAGES = ((0, 1, 2), (3, 5), (6, 7), (4,))


def index(h, z, x, c):
    return ((h % H * Z + z % Z) * X + x % X) * C + c


def devices():
    return [(h, z, x, c) for h in range(H) for z in range(Z) for x in range(X) for c in range(C)]


def groups():
    first = [[index(h, z, x, 0) for h in range(H) for x in range(X)] for z in range(Z)]
    second = [[index(h, z, x, 1) for z in range(Z)] for h in range(H) for x in range(X)]
    return first + second


def ring(step, cores=(0, 1)):
    pairs = []
    for h, z, x, c in devices():
        if c in cores:
            target = index(h, z + step, x, 0) if c == 0 else index(h, z, x + step, 1)
            pairs.append((index(h, z, x, c), target))
    return pairs


def across():
    pairs = []
    for h, z, x, c in devices():
        target = index(h, z + 4, x, 0) if c == 0 else index(h + 1, z, x, 1)
        pairs.append((index(h, z, x, c), target))
    return pairs


def across_core():
    return [(index(h, z, x, c), index(h, z, x, 1 - c)) for h, z, x, c in devices()]


def select_kernel(amp_ref, subset_ref, out_ref, copies_ref, amp_here, subset_here, sems):
    fetch = [
        pltpu.make_async_copy(amp_ref, amp_here, sems.at[8]),
        pltpu.make_async_copy(subset_ref, subset_here, sems.at[9]),
    ]
    for copy in fetch:
        copy.start()
    for copy in fetch:
        copy.wait()
    rows = amp_here.shape[1]
    hot = (lax.broadcasted_iota(jnp.int32, (rows, OCC), 0) == subset_here[...]).astype(jnp.bfloat16)
    out_ref[...] = jnp.dot(amp_here[...], hot, preferred_element_type=jnp.float32).astype(jnp.bfloat16)
    send_copies(out_ref, copies_ref, sems)


def select(amplitudes, subset):
    hbm, vmem = pl.BlockSpec(memory_space=pltpu.HBM), pl.BlockSpec(memory_space=pltpu.VMEM)
    return pl.pallas_call(
        select_kernel,
        out_shape=[
            jax.ShapeDtypeStruct((SHARD, OCC), jnp.bfloat16),
            jax.ShapeDtypeStruct((8 * SHARD, OCC), jnp.bfloat16),
        ],
        in_specs=[hbm, hbm],
        out_specs=[vmem, hbm],
        scratch_shapes=[
            pltpu.VMEM(amplitudes.shape, amplitudes.dtype),
            pltpu.VMEM(subset.shape, subset.dtype),
            pltpu.SemaphoreType.DMA((10,)),
        ],
        compiler_params=pltpu.CompilerParams(vmem_limit_bytes=VMEM_LIMIT),
        name="select",
    )(pltpu.with_memory_space_constraint(amplitudes, pltpu.HBM), pltpu.with_memory_space_constraint(subset, pltpu.HBM))


def send_copies(shard_ref, out_ref, sems):
    copies = [
        pltpu.make_async_copy(shard_ref, out_ref.at[pl.ds(copy * SHARD, SHARD), :], sems.at[copy]) for copy in range(8)
    ]
    for copy in copies:
        copy.start()
    for copy in copies:
        copy.wait()


def spread_kernel(shard_ref, out_ref, sems):
    send_copies(shard_ref, out_ref, sems)


def spread(shard):
    return pl.pallas_call(
        spread_kernel,
        out_shape=jax.ShapeDtypeStruct((8 * SHARD, OCC), jnp.bfloat16),
        in_specs=[pl.BlockSpec(memory_space=pltpu.VMEM)],
        out_specs=pl.BlockSpec(memory_space=pltpu.HBM),
        scratch_shapes=[pltpu.SemaphoreType.DMA((8,))],
        compiler_params=pltpu.CompilerParams(vmem_limit_bytes=VMEM_LIMIT),
        name="spread",
    )(shard)


def pick_kernel(core_ref, first_ref, second_ref, out_ref):
    @pl.when(core_ref[0] == 0)
    def _():
        out_ref[...] = first_ref[...]

    @pl.when(core_ref[0] == 1)
    def _():
        out_ref[...] = second_ref[...]


def pick(core, first, second):
    vmem = pl.BlockSpec(memory_space=pltpu.VMEM)
    return pl.pallas_call(
        pick_kernel,
        out_shape=jax.ShapeDtypeStruct(first.shape, first.dtype),
        in_specs=[pl.BlockSpec(memory_space=pltpu.SMEM), vmem, vmem],
        out_specs=vmem,
        compiler_params=pltpu.CompilerParams(vmem_limit_bytes=VMEM_LIMIT),
        name="pick",
    )(core, first, second)


def prepare_kernel(place_ref, ints_ref, low_ref, high_ref, *refs):
    out_refs, held_ref, sem = refs[: len(STAGES)], refs[-2], refs[-1]
    core = place_ref[64]
    start = place_ref[65]
    fetch = pltpu.make_async_copy(ints_ref.at[:, core], held_ref, sem)
    fetch.start()
    fetch.wait()
    low, high = low_ref[...], high_ref[...]
    for stage, numbers in enumerate(STAGES):
        for at, number in enumerate(numbers):
            parts = []
            for chunk in range(8):
                shard = place_ref[number * 8 + chunk]
                values = held_ref[shard]
                row = start + (2 * shard + core) * SHARD + lax.broadcasted_iota(jnp.int32, values.shape, 0)
                keep = (row >= low) & (row < high)
                parts.append(jnp.where(keep, values, jnp.zeros_like(values)))
            out_refs[stage][at] = jnp.concatenate(parts, axis=0).T


def prepare(place, ints, low, high):
    vmem = pl.BlockSpec(memory_space=pltpu.VMEM)
    return pl.pallas_call(
        prepare_kernel,
        out_shape=[jax.ShapeDtypeStruct((len(numbers), COLS, 512), jnp.bfloat16) for numbers in STAGES],
        in_specs=[pl.BlockSpec(memory_space=pltpu.SMEM), pl.BlockSpec(memory_space=pltpu.HBM), vmem, vmem],
        out_specs=[vmem] * len(STAGES),
        scratch_shapes=[pltpu.VMEM((64, SHARD, COLS), jnp.bfloat16), pltpu.SemaphoreType.DMA(())],
        compiler_params=pltpu.CompilerParams(vmem_limit_bytes=VMEM_LIMIT),
        cost_estimate=pl.CostEstimate(flops=0, bytes_accessed=6 << 20, transcendentals=0),
        name="prepare",
    )(place, pltpu.with_memory_space_constraint(ints, pltpu.HBM), low, high)


def early_kernel(count, fresh, near_ref, far_ref, *refs):
    pieces, out_ref = refs[:count], refs[-1]
    for half, masked_ref in enumerate((near_ref, far_ref)):
        rows = pl.ds(half * COLS, COLS)
        total = None if fresh else refs[-2][rows, :]
        for at in range(count):
            term = jnp.dot(masked_ref[at], pieces[at][...], preferred_element_type=jnp.float32)
            total = term if total is None else total + term
        out_ref[rows, :] = total


def early(near, far, pieces, before=None):
    vmem = pl.BlockSpec(memory_space=pltpu.VMEM)
    inputs = (near, far, *pieces) + (() if before is None else (before,))
    return pl.pallas_call(
        functools.partial(early_kernel, len(pieces), before is None),
        out_shape=jax.ShapeDtypeStruct((2 * COLS, OCC), jnp.float32),
        in_specs=[vmem] * len(inputs),
        out_specs=vmem,
        compiler_params=pltpu.CompilerParams(vmem_limit_bytes=VMEM_LIMIT),
        cost_estimate=pl.CostEstimate(
            flops=len(pieces) * 2 * 512**3, bytes_accessed=len(pieces) << 20, transcendentals=0
        ),
        name="early",
    )(*inputs)


def tail_kernel(near_ref, far_ref, piece_ref, before_ref, mine_ref, away_ref):
    for half, (masked_ref, out_ref) in enumerate(((near_ref, mine_ref), (far_ref, away_ref))):
        total = before_ref[pl.ds(half * COLS, COLS), :]
        total += jnp.dot(masked_ref[0], piece_ref[...], preferred_element_type=jnp.float32)
        for owner in range(GRP):
            out_ref[owner] = total[:, owner * OWN : (owner + 1) * OWN]


def tail(near, far, piece, before):
    vmem = pl.BlockSpec(memory_space=pltpu.VMEM)
    return pl.pallas_call(
        tail_kernel,
        out_shape=[jax.ShapeDtypeStruct((GRP, COLS, OWN), jnp.float32)] * 2,
        in_specs=[vmem] * 4,
        out_specs=[vmem] * 2,
        compiler_params=pltpu.CompilerParams(vmem_limit_bytes=VMEM_LIMIT),
        cost_estimate=pl.CostEstimate(flops=2 * 512**3, bytes_accessed=4 << 20, transcendentals=0),
        name="tail",
    )(near, far, piece, before)


def deal_kernel(me_ref, mine_ref, other_ref, *out_refs):
    me = me_ref[0]
    for step, out_ref in enumerate(out_refs):
        owner = me ^ step
        out_ref[...] = mine_ref[owner] + other_ref[owner]


def deal(me, mine, other):
    vmem = pl.BlockSpec(memory_space=pltpu.VMEM)
    return pl.pallas_call(
        deal_kernel,
        out_shape=[jax.ShapeDtypeStruct((COLS, OWN), jnp.float32)] * GRP,
        in_specs=[pl.BlockSpec(memory_space=pltpu.SMEM), vmem, vmem],
        out_specs=[vmem] * GRP,
        compiler_params=pltpu.CompilerParams(vmem_limit_bytes=VMEM_LIMIT),
        name="deal",
    )(me, mine, other)


def close_kernel(a_ref, b_ref, c_ref, d_ref, gap_ref, vir_ref, out_ref):
    total = a_ref[...] + b_ref[...] + c_ref[...] + d_ref[...]
    out_ref[...] = (total.T / (gap_ref[...] + vir_ref[...])).astype(jnp.bfloat16)


def close(terms, gaps, vir):
    vmem = pl.BlockSpec(memory_space=pltpu.VMEM)
    return pl.pallas_call(
        close_kernel,
        out_shape=jax.ShapeDtypeStruct((OWN, COLS), jnp.bfloat16),
        in_specs=[vmem] * 6,
        out_specs=vmem,
        compiler_params=pltpu.CompilerParams(vmem_limit_bytes=VMEM_LIMIT),
        name="close",
    )(*terms, gaps, vir)


def body(amplitudes, ladder_ints, pair_irrep, occ_gap, vir_energy, pair_subset):
    me = lax.axis_index("grp").astype(jnp.int32)
    blk = lax.axis_index("blk").astype(jnp.int32)
    c = blk % 2
    x = blk // 2 % X
    z = blk // 8 % Z
    h = blk // 64
    permute = functools.partial(lax.ppermute, axis_name="blk")

    amp = jnp.transpose(amplitudes[:, 0, :])
    shard, copies = select(amp, pair_subset[None, :])
    other_shard = permute(shard, perm=across())
    exchange = functools.partial(
        lax.all_to_all, axis_name="blk", split_axis=0, concat_axis=0, axis_index_groups=groups(), tiled=True
    )
    own = exchange(copies)
    pair_irrep, ints, copies = lax.optimization_barrier((pair_irrep, ladder_ints, copies))
    got = permute(ints, perm=across_core())

    t = jnp.arange(8, dtype=jnp.int32)
    z_from = [z, z - 1, z + 1, z - 2, z + 2, z + 4, z + 3, z - 3]
    zeros = [(t // 4 * Z + zz % Z) * X + t % 4 for zz in z_from]
    hx_from = [(h, x), (h, x - 1), (h, x + 1), (h, x - 2), (h + 1, x + 2), (h + 1, x), (h + 1, x - 1), (h + 1, x + 1)]
    ones = [(hh % H * Z + t) * X + xx % X for hh, xx in hx_from]
    shards = jnp.where(c == 0, jnp.concatenate(zeros), jnp.concatenate(ones))
    place = jnp.concatenate([shards, c[None], (me * QUARTER)[None]]).astype(jnp.int32)

    counts = jnp.sum((pair_irrep[None, :] < jnp.arange(9, dtype=jnp.int32)[:, None]).astype(jnp.int32), axis=1)
    labels = jnp.concatenate([
        lax.dynamic_slice_in_dim(pair_irrep, blk * COLS, COLS, 0),
        lax.dynamic_slice_in_dim(pair_irrep, (blk + 1 - 2 * c) * COLS, COLS, 0),
    ])
    is_label = labels[None, :] == jnp.arange(8, dtype=jnp.int32)[:, None]
    low = jnp.sum(jnp.where(is_label, counts[:8, None], 0), axis=0)[None, :]
    high = jnp.sum(jnp.where(is_label, counts[1:, None], 0), axis=0)[None, :]

    own = lax.all_to_all(copies, "blk", 0, 0, axis_index_groups=groups(), tiled=True)
    near = prepare(place, ladder_ints.reshape(64, 2, SHARD, COLS), low[:, :COLS], high[:, :COLS])
    other_shard, near = lax.optimization_barrier((other_shard, near))
    opposite = exchange(spread(other_shard))
    p1 = permute(own, perm=ring(1))
    m1 = permute(own, perm=ring(-1))
    p2 = permute(p1, perm=ring(1))
    m2 = permute(pick(c[None], m1, opposite), perm=ring(-1, (0,)) + ring(2, (1,)))
    p3 = permute(opposite, perm=ring(1))
    m3 = permute(opposite, perm=ring(-1))
    far = prepare(place, got.reshape(64, 2, SHARD, COLS), low[:, COLS:], high[:, COLS:])
    so_far = early(near[0], far[0], (own, p1, m1))
    so_far = early(near[1], far[1], (p2, opposite), so_far)
    so_far = early(near[2], far[2], (p3, m3), so_far)
    own_subset = lax.dynamic_slice_in_dim(pair_subset, me * OWN, OWN, 0)
    gaps = jnp.take(occ_gap, own_subset)
    so_far, gaps = lax.optimization_barrier((so_far, gaps))
    mine, away = tail(near[3], far[3], m2, so_far)
    other = permute(away, perm=across_core())
    dealt = deal(me[None], mine, other)
    terms = [dealt[0]]
    for step in (3, 2, 1):
        terms.append(lax.ppermute(dealt[step], "grp", [(i, i ^ step) for i in range(GRP)]))
    return close(terms, gaps[:, None], vir_energy[None, :])


def solution(mesh):
    return jax.shard_map(
        body,
        mesh=mesh,
        in_specs=(P(None, "grp", "blk"), P("grp", "blk"), P(), P(), P("blk"), P()),
        out_specs=P("grp", "blk"),
        check_vma=False,
    )
```

```python
import functools

import jax
import jax.numpy as jnp
from jax import lax
from jax.experimental import pallas as pl
from jax.experimental.pallas import tpu as pltpu
from jax.sharding import PartitionSpec as P

H, Z, X, C = 2, 8, 4, 2
SHARD = 64
OCC = 512
QUARTER = 8192
COLS = 256
GRP = 4
OWN = OCC // GRP
VMEM_LIMIT = 12 * 1024 * 1024
STAGES = ((0, 1, 2), (3, 5), (7, 6), (4,))


def index(h, z, x, c):
    return ((h % H * Z + z % Z) * X + x % X) * C + c


def devices():
    return [(h, z, x, c) for h in range(H) for z in range(Z) for x in range(X) for c in range(C)]


def groups():
    first = [[index(h, z, x, 0) for h in range(H) for x in range(X)] for z in range(Z)]
    second = [[index(h, z, x, 1) for z in range(Z)] for h in range(H) for x in range(X)]
    return first + second


def ring(step, cores=(0, 1)):
    pairs = []
    for h, z, x, c in devices():
        if c in cores:
            target = index(h, z + step, x, 0) if c == 0 else index(h, z, x + step, 1)
            pairs.append((index(h, z, x, c), target))
    return pairs


def across():
    pairs = []
    for h, z, x, c in devices():
        target = index(h, z + 4, x, 0) if c == 0 else index(h + 1, z, x, 1)
        pairs.append((index(h, z, x, c), target))
    return pairs


def across_core():
    return [(index(h, z, x, c), index(h, z, x, 1 - c)) for h, z, x, c in devices()]


def select_kernel(amp_ref, subset_ref, copies_ref, amp_here, subset_here, shard_ref, sems):
    fetch = [
        pltpu.make_async_copy(amp_ref, amp_here, sems.at[8]),
        pltpu.make_async_copy(subset_ref, subset_here, sems.at[9]),
    ]
    for copy in fetch:
        copy.start()
    for copy in fetch:
        copy.wait()
    rows = amp_here.shape[1]
    hot = (lax.broadcasted_iota(jnp.int32, (rows, OCC), 0) == subset_here[...]).astype(jnp.bfloat16)
    shard_ref[...] = jnp.dot(amp_here[...], hot, preferred_element_type=jnp.float32).astype(jnp.bfloat16)
    copies = [
        pltpu.make_async_copy(shard_ref, copies_ref.at[pl.ds(copy * SHARD, SHARD), :], sems.at[copy])
        for copy in range(8)
    ]
    for copy in copies:
        copy.start()
    for copy in copies:
        copy.wait()


def select(amplitudes, subset):
    hbm = pl.BlockSpec(memory_space=pltpu.HBM)
    return pl.pallas_call(
        select_kernel,
        out_shape=jax.ShapeDtypeStruct((8 * SHARD, OCC), jnp.bfloat16),
        in_specs=[hbm, hbm],
        out_specs=hbm,
        scratch_shapes=[
            pltpu.VMEM(amplitudes.shape, amplitudes.dtype),
            pltpu.VMEM(subset.shape, subset.dtype),
            pltpu.VMEM((SHARD, OCC), jnp.bfloat16),
            pltpu.SemaphoreType.DMA((10,)),
        ],
        compiler_params=pltpu.CompilerParams(vmem_limit_bytes=VMEM_LIMIT),
        name="select",
    )(pltpu.with_memory_space_constraint(amplitudes, pltpu.HBM), pltpu.with_memory_space_constraint(subset, pltpu.HBM))


def pick_kernel(core_ref, first_ref, second_ref, out_ref):
    @pl.when(core_ref[0] == 0)
    def _():
        out_ref[...] = first_ref[...]

    @pl.when(core_ref[0] == 1)
    def _():
        out_ref[...] = second_ref[...]


def pick(core, first, second):
    vmem = pl.BlockSpec(memory_space=pltpu.VMEM)
    return pl.pallas_call(
        pick_kernel,
        out_shape=jax.ShapeDtypeStruct(first.shape, first.dtype),
        in_specs=[pl.BlockSpec(memory_space=pltpu.SMEM), vmem, vmem],
        out_specs=vmem,
        compiler_params=pltpu.CompilerParams(vmem_limit_bytes=VMEM_LIMIT),
        name="pick",
    )(core, first, second)


def prepare_kernel(place_ref, ints_ref, low_ref, high_ref, *refs):
    out_refs, held_ref, sem = refs[: len(STAGES)], refs[-2], refs[-1]
    core = place_ref[64]
    start = place_ref[65]
    fetch = pltpu.make_async_copy(ints_ref.at[:, core], held_ref, sem)
    fetch.start()
    fetch.wait()
    low, high = low_ref[...], high_ref[...]
    for stage, numbers in enumerate(STAGES):
        for at, number in enumerate(numbers):
            parts = []
            for chunk in range(8):
                shard = place_ref[number * 8 + chunk]
                values = held_ref[shard]
                row = start + (2 * shard + core) * SHARD + lax.broadcasted_iota(jnp.int32, values.shape, 0)
                keep = (row >= low) & (row < high)
                parts.append(jnp.where(keep, values, jnp.zeros_like(values)))
            out_refs[stage][at] = jnp.concatenate(parts, axis=0).T


def prepare(place, ints, low, high):
    vmem = pl.BlockSpec(memory_space=pltpu.VMEM)
    return pl.pallas_call(
        prepare_kernel,
        out_shape=[jax.ShapeDtypeStruct((len(numbers), COLS, 512), jnp.bfloat16) for numbers in STAGES],
        in_specs=[pl.BlockSpec(memory_space=pltpu.SMEM), pl.BlockSpec(memory_space=pltpu.HBM), vmem, vmem],
        out_specs=[vmem] * len(STAGES),
        scratch_shapes=[pltpu.VMEM((64, SHARD, COLS), jnp.bfloat16), pltpu.SemaphoreType.DMA(())],
        compiler_params=pltpu.CompilerParams(vmem_limit_bytes=VMEM_LIMIT),
        cost_estimate=pl.CostEstimate(flops=0, bytes_accessed=6 << 20, transcendentals=0),
        name="prepare",
    )(place, pltpu.with_memory_space_constraint(ints, pltpu.HBM), low, high)


def early_kernel(count, fresh, near_ref, far_ref, *refs):
    pieces, out_ref = refs[:count], refs[-1]
    for half, masked_ref in enumerate((near_ref, far_ref)):
        rows = pl.ds(half * COLS, COLS)
        total = None if fresh else refs[-2][rows, :]
        for at in range(count):
            term = jnp.dot(masked_ref[at], pieces[at][...], preferred_element_type=jnp.float32)
            total = term if total is None else total + term
        out_ref[rows, :] = total


def early(near, far, pieces, before=None):
    vmem = pl.BlockSpec(memory_space=pltpu.VMEM)
    inputs = (near, far, *pieces) + (() if before is None else (before,))
    return pl.pallas_call(
        functools.partial(early_kernel, len(pieces), before is None),
        out_shape=jax.ShapeDtypeStruct((2 * COLS, OCC), jnp.float32),
        in_specs=[vmem] * len(inputs),
        out_specs=vmem,
        compiler_params=pltpu.CompilerParams(vmem_limit_bytes=VMEM_LIMIT),
        cost_estimate=pl.CostEstimate(
            flops=len(pieces) * 2 * 512**3, bytes_accessed=len(pieces) << 20, transcendentals=0
        ),
        name="early",
    )(*inputs)


def tail_kernel(near_ref, far_ref, piece_ref, before_ref, mine_ref, away_ref):
    for half, (masked_ref, out_ref) in enumerate(((near_ref, mine_ref), (far_ref, away_ref))):
        total = before_ref[pl.ds(half * COLS, COLS), :]
        total += jnp.dot(masked_ref[0], piece_ref[...], preferred_element_type=jnp.float32)
        for owner in range(GRP):
            out_ref[owner] = total[:, owner * OWN : (owner + 1) * OWN]


def tail(near, far, piece, before):
    vmem = pl.BlockSpec(memory_space=pltpu.VMEM)
    return pl.pallas_call(
        tail_kernel,
        out_shape=[jax.ShapeDtypeStruct((GRP, COLS, OWN), jnp.float32)] * 2,
        in_specs=[vmem] * 4,
        out_specs=[vmem] * 2,
        compiler_params=pltpu.CompilerParams(vmem_limit_bytes=VMEM_LIMIT),
        cost_estimate=pl.CostEstimate(flops=2 * 512**3, bytes_accessed=4 << 20, transcendentals=0),
        name="tail",
    )(near, far, piece, before)


def deal_kernel(me_ref, mine_ref, other_ref, *out_refs):
    me = me_ref[0]
    for step, out_ref in enumerate(out_refs):
        owner = me ^ step
        out_ref[...] = mine_ref[owner] + other_ref[owner]


def deal(me, mine, other):
    vmem = pl.BlockSpec(memory_space=pltpu.VMEM)
    return pl.pallas_call(
        deal_kernel,
        out_shape=[jax.ShapeDtypeStruct((COLS, OWN), jnp.float32)] * GRP,
        in_specs=[pl.BlockSpec(memory_space=pltpu.SMEM), vmem, vmem],
        out_specs=[vmem] * GRP,
        compiler_params=pltpu.CompilerParams(vmem_limit_bytes=VMEM_LIMIT),
        name="deal",
    )(me, mine, other)


def close_kernel(a_ref, b_ref, c_ref, d_ref, gap_ref, vir_ref, out_ref):
    total = a_ref[...] + b_ref[...] + c_ref[...] + d_ref[...]
    out_ref[...] = (total.T / (gap_ref[...] + vir_ref[...])).astype(jnp.bfloat16)


def close(terms, gaps, vir):
    vmem = pl.BlockSpec(memory_space=pltpu.VMEM)
    return pl.pallas_call(
        close_kernel,
        out_shape=jax.ShapeDtypeStruct((OWN, COLS), jnp.bfloat16),
        in_specs=[vmem] * 6,
        out_specs=vmem,
        compiler_params=pltpu.CompilerParams(vmem_limit_bytes=VMEM_LIMIT),
        name="close",
    )(*terms, gaps, vir)


def body(amplitudes, ladder_ints, pair_irrep, occ_gap, vir_energy, pair_subset):
    me = lax.axis_index("grp").astype(jnp.int32)
    blk = lax.axis_index("blk").astype(jnp.int32)
    c = blk % 2
    x = blk // 2 % X
    z = blk // 8 % Z
    h = blk // 64
    permute = functools.partial(lax.ppermute, axis_name="blk")

    amp = jnp.transpose(amplitudes[:, 0, :])
    copies = select(amp, pair_subset[None, :])
    exchange = functools.partial(
        lax.all_to_all, axis_name="blk", split_axis=0, concat_axis=0, axis_index_groups=groups(), tiled=True
    )
    own = exchange(copies)
    pair_irrep, ints, copies = lax.optimization_barrier((pair_irrep, ladder_ints, copies))
    got = permute(ints, perm=across_core())

    t = jnp.arange(8, dtype=jnp.int32)
    z_from = [z, z - 1, z + 1, z - 2, z + 2, z + 4, z + 3, z - 3]
    zeros = [(t // 4 * Z + zz % Z) * X + t % 4 for zz in z_from]
    hx_from = [(h, x), (h, x - 1), (h, x + 1), (h, x - 2), (h + 1, x + 2), (h + 1, x), (h + 1, x - 1), (h + 1, x + 1)]
    ones = [(hh % H * Z + t) * X + xx % X for hh, xx in hx_from]
    shards = jnp.where(c == 0, jnp.concatenate(zeros), jnp.concatenate(ones))
    place = jnp.concatenate([shards, c[None], (me * QUARTER)[None]]).astype(jnp.int32)

    counts = jnp.sum((pair_irrep[None, :] < jnp.arange(9, dtype=jnp.int32)[:, None]).astype(jnp.int32), axis=1)
    labels = jnp.concatenate([
        lax.dynamic_slice_in_dim(pair_irrep, blk * COLS, COLS, 0),
        lax.dynamic_slice_in_dim(pair_irrep, (blk + 1 - 2 * c) * COLS, COLS, 0),
    ])
    is_label = labels[None, :] == jnp.arange(8, dtype=jnp.int32)[:, None]
    low = jnp.sum(jnp.where(is_label, counts[:8, None], 0), axis=0)[None, :]
    high = jnp.sum(jnp.where(is_label, counts[1:, None], 0), axis=0)[None, :]

    own = lax.all_to_all(copies, "blk", 0, 0, axis_index_groups=groups(), tiled=True)
    near = prepare(place, ladder_ints.reshape(64, 2, SHARD, COLS), low[:, :COLS], high[:, :COLS])
    own, near = lax.optimization_barrier((own, near))
    opposite = permute(own, perm=across())
    far = prepare(place, got.reshape(64, 2, SHARD, COLS), low[:, COLS:], high[:, COLS:])
    own_subset = lax.dynamic_slice_in_dim(pair_subset, me * OWN, OWN, 0)
    gaps = jnp.take(occ_gap, own_subset)
    opposite, far, gaps = lax.optimization_barrier((opposite, far, gaps))
    p1 = permute(own, perm=ring(1))
    m1 = permute(own, perm=ring(-1))
    p2 = permute(p1, perm=ring(1))
    m2 = permute(pick(c[None], m1, opposite), perm=ring(-1, (0,)) + ring(2, (1,)))
    m3 = permute(opposite, perm=ring(-1))
    p3 = permute(opposite, perm=ring(1))
    so_far = early(near[0], far[0], (own, p1, m1))
    so_far = early(near[1], far[1], (p2, opposite), so_far)
    so_far = early(near[2], far[2], (m3, p3), so_far)
    mine, away = tail(near[3], far[3], m2, so_far)
    other = permute(away, perm=across_core())
    dealt = deal(me[None], mine, other)
    terms = [dealt[0]]
    for step in (3, 2, 1):
        terms.append(lax.ppermute(dealt[step], "grp", [(i, i ^ step) for i in range(GRP)]))
    return close(terms, gaps[:, None], vir_energy[None, :])


def solution(mesh):
    return jax.shard_map(
        body,
        mesh=mesh,
        in_specs=(P(None, "grp", "blk"), P("grp", "blk"), P(), P(), P("blk"), P()),
        out_specs=P("grp", "blk"),
        check_vma=False,
    )
```

```python
import functools

import jax
import jax.numpy as jnp
from jax import lax
from jax.experimental import pallas as pl
from jax.experimental.pallas import tpu as pltpu
from jax.sharding import PartitionSpec as P

H, Z, X, C = 2, 8, 4, 2
SHARD = 64
OCC = 512
QUARTER = 8192
COLS = 256
GRP = 4
OWN = OCC // GRP
VMEM_LIMIT = 12 * 1024 * 1024
STAGES = ((0, 1, 2), (3, 5), (7, 6), (4,))


def index(h, z, x, c):
    return ((h % H * Z + z % Z) * X + x % X) * C + c


def devices():
    return [(h, z, x, c) for h in range(H) for z in range(Z) for x in range(X) for c in range(C)]


def groups():
    first = [[index(h, z, x, 0) for h in range(H) for x in range(X)] for z in range(Z)]
    second = [[index(h, z, x, 1) for z in range(Z)] for h in range(H) for x in range(X)]
    return first + second


def ring(step, cores=(0, 1)):
    pairs = []
    for h, z, x, c in devices():
        if c in cores:
            target = index(h, z + step, x, 0) if c == 0 else index(h, z, x + step, 1)
            pairs.append((index(h, z, x, c), target))
    return pairs


def across():
    pairs = []
    for h, z, x, c in devices():
        target = index(h, z + 4, x, 0) if c == 0 else index(h + 1, z, x, 1)
        pairs.append((index(h, z, x, c), target))
    return pairs


def across_core():
    return [(index(h, z, x, c), index(h, z, x, 1 - c)) for h, z, x, c in devices()]


def select_kernel(amp_ref, subset_ref, copies_ref, amp_here, subset_here, shard_ref, sems):
    fetch = [
        pltpu.make_async_copy(amp_ref, amp_here, sems.at[8]),
        pltpu.make_async_copy(subset_ref, subset_here, sems.at[9]),
    ]
    for copy in fetch:
        copy.start()
    fetch[1].wait()
    rows = amp_here.shape[1]
    hot = (lax.broadcasted_iota(jnp.int32, (rows, OCC), 0) == subset_here[...]).astype(jnp.bfloat16)
    fetch[0].wait()
    shard_ref[...] = jnp.dot(amp_here[...], hot, preferred_element_type=jnp.float32).astype(jnp.bfloat16)
    copies = [
        pltpu.make_async_copy(shard_ref, copies_ref.at[pl.ds(copy * SHARD, SHARD), :], sems.at[copy])
        for copy in range(8)
    ]
    for copy in copies:
        copy.start()
    for copy in copies:
        copy.wait()


def select(amplitudes, subset):
    hbm = pl.BlockSpec(memory_space=pltpu.HBM)
    return pl.pallas_call(
        select_kernel,
        out_shape=jax.ShapeDtypeStruct((8 * SHARD, OCC), jnp.bfloat16),
        in_specs=[hbm, hbm],
        out_specs=hbm,
        scratch_shapes=[
            pltpu.VMEM(amplitudes.shape, amplitudes.dtype),
            pltpu.VMEM(subset.shape, subset.dtype),
            pltpu.VMEM((SHARD, OCC), jnp.bfloat16),
            pltpu.SemaphoreType.DMA((10,)),
        ],
        compiler_params=pltpu.CompilerParams(vmem_limit_bytes=VMEM_LIMIT),
        name="select",
    )(pltpu.with_memory_space_constraint(amplitudes, pltpu.HBM), pltpu.with_memory_space_constraint(subset, pltpu.HBM))


def pick_kernel(core_ref, first_ref, second_ref, out_ref):
    @pl.when(core_ref[0] == 0)
    def _():
        out_ref[...] = first_ref[...]

    @pl.when(core_ref[0] == 1)
    def _():
        out_ref[...] = second_ref[...]


def pick(core, first, second):
    vmem = pl.BlockSpec(memory_space=pltpu.VMEM)
    return pl.pallas_call(
        pick_kernel,
        out_shape=jax.ShapeDtypeStruct(first.shape, first.dtype),
        in_specs=[pl.BlockSpec(memory_space=pltpu.SMEM), vmem, vmem],
        out_specs=vmem,
        compiler_params=pltpu.CompilerParams(vmem_limit_bytes=VMEM_LIMIT),
        name="pick",
    )(core, first, second)


def prepare_kernel(place_ref, ints_ref, low_ref, high_ref, *refs):
    out_refs, held_ref, sem = refs[: len(STAGES)], refs[-2], refs[-1]
    core = place_ref[64]
    start = place_ref[65]
    fetch = pltpu.make_async_copy(ints_ref.at[:, core], held_ref, sem)
    fetch.start()
    fetch.wait()
    low, high = low_ref[...], high_ref[...]
    for stage, numbers in enumerate(STAGES):
        for at, number in enumerate(numbers):
            parts = []
            for chunk in range(8):
                shard = place_ref[number * 8 + chunk]
                values = held_ref[shard]
                row = start + (2 * shard + core) * SHARD + lax.broadcasted_iota(jnp.int32, values.shape, 0)
                keep = (row >= low) & (row < high)
                parts.append(jnp.where(keep, values, jnp.zeros_like(values)))
            out_refs[stage][at] = jnp.concatenate(parts, axis=0).T


def prepare(place, ints, low, high):
    vmem = pl.BlockSpec(memory_space=pltpu.VMEM)
    return pl.pallas_call(
        prepare_kernel,
        out_shape=[jax.ShapeDtypeStruct((len(numbers), COLS, 512), jnp.bfloat16) for numbers in STAGES],
        in_specs=[pl.BlockSpec(memory_space=pltpu.SMEM), pl.BlockSpec(memory_space=pltpu.HBM), vmem, vmem],
        out_specs=[vmem] * len(STAGES),
        scratch_shapes=[pltpu.VMEM((64, SHARD, COLS), jnp.bfloat16), pltpu.SemaphoreType.DMA(())],
        compiler_params=pltpu.CompilerParams(vmem_limit_bytes=VMEM_LIMIT),
        cost_estimate=pl.CostEstimate(flops=0, bytes_accessed=6 << 20, transcendentals=0),
        name="prepare",
    )(place, pltpu.with_memory_space_constraint(ints, pltpu.HBM), low, high)


def early_kernel(count, fresh, near_ref, far_ref, *refs):
    pieces, out_ref = refs[:count], refs[-1]
    for half, masked_ref in enumerate((near_ref, far_ref)):
        rows = pl.ds(half * COLS, COLS)
        total = None if fresh else refs[-2][rows, :]
        for at in range(count):
            term = jnp.dot(masked_ref[at], pieces[at][...], preferred_element_type=jnp.float32)
            total = term if total is None else total + term
        out_ref[rows, :] = total


def early(near, far, pieces, before=None):
    vmem = pl.BlockSpec(memory_space=pltpu.VMEM)
    inputs = (near, far, *pieces) + (() if before is None else (before,))
    return pl.pallas_call(
        functools.partial(early_kernel, len(pieces), before is None),
        out_shape=jax.ShapeDtypeStruct((2 * COLS, OCC), jnp.float32),
        in_specs=[vmem] * len(inputs),
        out_specs=vmem,
        compiler_params=pltpu.CompilerParams(vmem_limit_bytes=VMEM_LIMIT),
        cost_estimate=pl.CostEstimate(
            flops=len(pieces) * 2 * 512**3, bytes_accessed=len(pieces) << 20, transcendentals=0
        ),
        name="early",
    )(*inputs)


def tail_kernel(near_ref, far_ref, piece_ref, before_ref, mine_ref, away_ref):
    for half, (masked_ref, out_ref) in enumerate(((near_ref, mine_ref), (far_ref, away_ref))):
        total = before_ref[pl.ds(half * COLS, COLS), :]
        total += jnp.dot(masked_ref[0], piece_ref[...], preferred_element_type=jnp.float32)
        for owner in range(GRP):
            out_ref[owner] = total[:, owner * OWN : (owner + 1) * OWN]


def tail(near, far, piece, before):
    vmem = pl.BlockSpec(memory_space=pltpu.VMEM)
    return pl.pallas_call(
        tail_kernel,
        out_shape=[jax.ShapeDtypeStruct((GRP, COLS, OWN), jnp.float32)] * 2,
        in_specs=[vmem] * 4,
        out_specs=[vmem] * 2,
        compiler_params=pltpu.CompilerParams(vmem_limit_bytes=VMEM_LIMIT),
        cost_estimate=pl.CostEstimate(flops=2 * 512**3, bytes_accessed=4 << 20, transcendentals=0),
        name="tail",
    )(near, far, piece, before)


def deal_kernel(me_ref, mine_ref, other_ref, *out_refs):
    me = me_ref[0]
    for step, out_ref in enumerate(out_refs):
        owner = me ^ step
        out_ref[...] = mine_ref[owner] + other_ref[owner]


def deal(me, mine, other):
    vmem = pl.BlockSpec(memory_space=pltpu.VMEM)
    return pl.pallas_call(
        deal_kernel,
        out_shape=[jax.ShapeDtypeStruct((COLS, OWN), jnp.float32)] * GRP,
        in_specs=[pl.BlockSpec(memory_space=pltpu.SMEM), vmem, vmem],
        out_specs=[vmem] * GRP,
        compiler_params=pltpu.CompilerParams(vmem_limit_bytes=VMEM_LIMIT),
        name="deal",
    )(me, mine, other)


def close_kernel(a_ref, b_ref, c_ref, d_ref, gap_ref, vir_ref, out_ref):
    total = a_ref[...] + b_ref[...] + c_ref[...] + d_ref[...]
    out_ref[...] = (total.T / (gap_ref[...] + vir_ref[...])).astype(jnp.bfloat16)


def close(terms, gaps, vir):
    vmem = pl.BlockSpec(memory_space=pltpu.VMEM)
    return pl.pallas_call(
        close_kernel,
        out_shape=jax.ShapeDtypeStruct((OWN, COLS), jnp.bfloat16),
        in_specs=[vmem] * 6,
        out_specs=vmem,
        compiler_params=pltpu.CompilerParams(vmem_limit_bytes=VMEM_LIMIT),
        name="close",
    )(*terms, gaps, vir)


def body(amplitudes, ladder_ints, pair_irrep, occ_gap, vir_energy, pair_subset):
    me = lax.axis_index("grp").astype(jnp.int32)
    blk = lax.axis_index("blk").astype(jnp.int32)
    c = blk % 2
    x = blk // 2 % X
    z = blk // 8 % Z
    h = blk // 64
    permute = functools.partial(lax.ppermute, axis_name="blk")

    amp = jnp.transpose(amplitudes[:, 0, :])
    copies = select(amp, pair_subset[None, :])
    exchange = functools.partial(
        lax.all_to_all, axis_name="blk", split_axis=0, concat_axis=0, axis_index_groups=groups(), tiled=True
    )
    own = exchange(copies)
    pair_irrep, copies = lax.optimization_barrier((pair_irrep, copies))

    t = jnp.arange(8, dtype=jnp.int32)
    z_from = [z, z - 1, z + 1, z - 2, z + 2, z + 4, z + 3, z - 3]
    zeros = [(t // 4 * Z + zz % Z) * X + t % 4 for zz in z_from]
    hx_from = [(h, x), (h, x - 1), (h, x + 1), (h, x - 2), (h + 1, x + 2), (h + 1, x), (h + 1, x - 1), (h + 1, x + 1)]
    ones = [(hh % H * Z + t) * X + xx % X for hh, xx in hx_from]
    shards = jnp.where(c == 0, jnp.concatenate(zeros), jnp.concatenate(ones))
    place = jnp.concatenate([shards, c[None], (me * QUARTER)[None]]).astype(jnp.int32)

    counts = jnp.sum((pair_irrep[None, :] < jnp.arange(9, dtype=jnp.int32)[:, None]).astype(jnp.int32), axis=1)
    labels = jnp.concatenate([
        lax.dynamic_slice_in_dim(pair_irrep, blk * COLS, COLS, 0),
        lax.dynamic_slice_in_dim(pair_irrep, (blk + 1 - 2 * c) * COLS, COLS, 0),
    ])
    is_label = labels[None, :] == jnp.arange(8, dtype=jnp.int32)[:, None]
    low = jnp.sum(jnp.where(is_label, counts[:8, None], 0), axis=0)[None, :]
    high = jnp.sum(jnp.where(is_label, counts[1:, None], 0), axis=0)[None, :]

    own = lax.all_to_all(copies, "blk", 0, 0, axis_index_groups=groups(), tiled=True)
    near = prepare(place, ladder_ints.reshape(64, 2, SHARD, COLS), low[:, :COLS], high[:, :COLS])
    own, near, ints = lax.optimization_barrier((own, near, ladder_ints))
    got = permute(ints, perm=across_core())
    opposite = permute(own, perm=across())
    far = prepare(place, got.reshape(64, 2, SHARD, COLS), low[:, COLS:], high[:, COLS:])
    own_subset = lax.dynamic_slice_in_dim(pair_subset, me * OWN, OWN, 0)
    gaps = jnp.take(occ_gap, own_subset)
    opposite, far, gaps = lax.optimization_barrier((opposite, far, gaps))
    p1 = permute(own, perm=ring(1))
    m1 = permute(own, perm=ring(-1))
    p2 = permute(p1, perm=ring(1))
    m2 = permute(pick(c[None], m1, opposite), perm=ring(-1, (0,)) + ring(2, (1,)))
    m3 = permute(opposite, perm=ring(-1))
    p3 = permute(opposite, perm=ring(1))
    so_far = early(near[0], far[0], (own, p1, m1))
    so_far = early(near[1], far[1], (p2, opposite), so_far)
    so_far = early(near[2], far[2], (m3, p3), so_far)
    mine, away = tail(near[3], far[3], m2, so_far)
    other = permute(away, perm=across_core())
    dealt = deal(me[None], mine, other)
    terms = [dealt[0]]
    for step in (3, 2, 1):
        terms.append(lax.ppermute(dealt[step], "grp", [(i, i ^ step) for i in range(GRP)]))
    return close(terms, gaps[:, None], vir_energy[None, :])


def solution(mesh):
    return jax.shard_map(
        body,
        mesh=mesh,
        in_specs=(P(None, "grp", "blk"), P("grp", "blk"), P(), P(), P("blk"), P()),
        out_specs=P("grp", "blk"),
        check_vma=False,
    )
```
